512 devices in a mesh: lon: 16 (over z, core), lat: 32 (over y, x).
Axes of the slice: x: 4, y: 8, z: 8, core: 2. Of those that a mesh axis runs over, the one named last changes fastest.
Arguments:
- increment: float32 [2, 64, 768, 2048], P(None, None, 'lat', 'lon'), may hold values from -6 to 6
- eastward_rate: float32 [2, 64, 768], P(None, None, 'lat'), as said below
- eastward_spike: float32 [768, 2048], P('lat', 'lon'), as said below
- northward_rate: float32 [2, 64, 768], replicated, as said below
- vertical: float32 [2, 64, 64], replicated, may hold values from -0.75 to 0.75
Outputs:
- correlated: float32 [2, 64, 768, 2048], P(None, None, 'lat', 'lon')
The draws below stay inside these ranges and needn't reach their ends.
Inputs may be any that keep to these rules, and one draw needn't show every extreme that they name: `eastward_rate`: every entry is positive and below 1. `eastward_spike`: every entry is positive and at most 1. `northward_rate`: every entry is positive and below 1.
All inputs are finite; a program needn't handle non-finite values.
Results may differ from the reference program's by a relative error of at most 0.0003.
Values sent between devices are 32-bit elements; how exact they have to be, the bound alone decides.
A program may use at most 64 MiB of HBM per device.

```python
import jax
import jax.numpy as jnp
from jax import lax

CONTROL_COUNT = 2
VERTICAL_LEVELS = 64
LATITUDE_ROWS = 768
LONGITUDE_COLUMNS = 2048


def decay_rows(key, row_shape, length):
    initial_key, middle_key, final_key = jax.random.split(key, 3)
    slow_share = 0.5
    slow_rows = jax.random.uniform(initial_key, row_shape) < slow_share
    slow_rate = jnp.exp(-jax.random.uniform(middle_key, row_shape, minval=0.3, maxval=1.0) / length)
    fast_rate = jnp.exp(-1.0 / jax.random.uniform(final_key, row_shape, minval=30.0, maxval=50.0))
    return jnp.where(slow_rows, slow_rate, fast_rate).astype(jnp.float32)


def draw_eastward_rate(key, part):
    return decay_rows(jax.random.fold_in(key, 11), (CONTROL_COUNT, VERTICAL_LEVELS, LATITUDE_ROWS), LONGITUDE_COLUMNS)


def draw_eastward_spike(key, part):
    initial_key, middle_key = jax.random.split(jax.random.fold_in(key, 23))
    spike_trigger = jax.random.uniform(initial_key, (LATITUDE_ROWS, LONGITUDE_COLUMNS)) < 2.0 / LONGITUDE_COLUMNS
    spike_cutoff = jax.random.uniform(middle_key, (LATITUDE_ROWS, LONGITUDE_COLUMNS), minval=0.6, maxval=0.8)
    return jnp.where(spike_trigger, spike_cutoff, 1.0).astype(jnp.float32)


def draw_northward_rate(key, part):
    initial_key, middle_key, final_key = jax.random.split(jax.random.fold_in(key, 37), 3)
    baseline_rate = decay_rows(initial_key, (CONTROL_COUNT, VERTICAL_LEVELS, 1), LATITUDE_ROWS)
    spike_trigger = jax.random.uniform(middle_key, (CONTROL_COUNT, VERTICAL_LEVELS, LATITUDE_ROWS)) < 2.0 / LATITUDE_ROWS
    spike_cutoff = jax.random.uniform(final_key, (CONTROL_COUNT, VERTICAL_LEVELS, LATITUDE_ROWS), minval=0.6, maxval=0.8)
    return (baseline_rate * jnp.where(spike_trigger, spike_cutoff, 1.0)).astype(jnp.float32)


def level_of(rng, shape, cuts, least, largest):
    loudness = 1.0
    for dim, shards_of in cuts:
        steps = jax.random.uniform(jax.random.fold_in(jax.random.fold_in(rng, 6), dim), (shards_of,), jnp.float32, least / len(cuts), largest / len(cuts))
        loudness = loudness * jnp.repeat(jnp.exp(steps), shape[dim] // shards_of).reshape((-1,) + (1,) * (len(shape) - 1 - dim))
    return loudness


def normal_values(key, dims, deviation, bound, cuts=(), dtype=jnp.bfloat16):
    values = jax.random.normal(key, dims, jnp.float32) * deviation
    if len(cuts) > 0:
        values = level_of(key, dims, cuts, -0.22, 0.18) * values
    return jnp.clip(values, min=-bound, max=bound).astype(dtype)


def setup_inputs(seed: int = 0) -> dict:
    streams_of = jax.random.split(jax.random.key(seed), 6)
    increment = normal_values(streams_of[0], (CONTROL_COUNT, VERTICAL_LEVELS, LATITUDE_ROWS, LONGITUDE_COLUMNS), 1.0, 6.0, ((2, 32), (3, 16)), jnp.float32)
    eastward_rate = draw_eastward_rate(jax.random.fold_in(streams_of[5], 71), 0)
    eastward_spike = draw_eastward_spike(jax.random.fold_in(streams_of[5], 71), 0)
    northward_rate = draw_northward_rate(jax.random.fold_in(streams_of[5], 71), 0)
    vertical = normal_values(streams_of[4], (CONTROL_COUNT, VERTICAL_LEVELS, VERTICAL_LEVELS), VERTICAL_LEVELS ** -0.5, 0.75, (), jnp.float32)
    return dict(increment=increment, eastward_rate=eastward_rate, eastward_spike=eastward_spike, northward_rate=northward_rate, vertical=vertical)


def compose(earlier, following):
    return (following[0] * earlier[0], following[1] + following[0] * earlier[1])

def eastward_sweep(field_per_level, eastward_rows, eastward_spike):
    decay_factors = eastward_rows[:, None] * eastward_spike
    factor, local_part = lax.associative_scan(compose, (decay_factors, field_per_level), reverse=True, axis=1)
    wrapped = local_part[:, 0] / (1.0 - factor[:, 0])
    return jnp.sqrt(1.0 - decay_factors * decay_factors) * (local_part + factor * wrapped[:, None])

def meridional_pass(field_per_level, meridional_rows):
    rate_grid = jnp.broadcast_to(meridional_rows[:, None], field_per_level.shape)
    growth, filtered = lax.associative_scan(compose, (rate_grid, field_per_level), axis=0)
    return jnp.sqrt(1.0 - rate_grid * rate_grid) * filtered

def reference(increment, eastward_rate, eastward_spike, northward_rate, vertical):
    flattened = increment.reshape((CONTROL_COUNT * VERTICAL_LEVELS, LATITUDE_ROWS, LONGITUDE_COLUMNS))
    eastward_rows = eastward_rate.reshape((CONTROL_COUNT * VERTICAL_LEVELS, LATITUDE_ROWS))
    meridional_rows = northward_rate.reshape((CONTROL_COUNT * VERTICAL_LEVELS, LATITUDE_ROWS))

    def one_level(operands):
        field_per_level, eastward_current, meridional_here = operands
        eastward_output = eastward_sweep(field_per_level, eastward_current, eastward_spike)
        return meridional_pass(eastward_output, meridional_here)
    mixed = lax.map(one_level, (flattened, eastward_rows, meridional_rows)).reshape(increment.shape)
    return jnp.einsum('vlk,vlab->vkab', vertical, mixed, precision=lax.Precision.HIGHEST)
```

```python
import jax
import jax.numpy as jnp
from jax import lax
from jax.experimental import pallas as pl
from jax.experimental.pallas import tpu as pltpu
from jax.sharding import PartitionSpec as P

V, L, J, I = 2, 64, 24, 128
LON, LAT = 16, 32
MESH = pl.DeviceIdType.MESH
f32 = jnp.float32


def lanes(rows):
    return lax.broadcasted_iota(jnp.int32, (rows, I), 1)


def left(x, n):
    size = x.shape[1]
    return pltpu.roll(x, size - n, 1) if n else x


def root(x):
    return x * lax.rsqrt(jnp.maximum(x, 1e-30))


def column(x, j):
    return jnp.broadcast_to(x[:, j : j + 1], (x.shape[0], I))


def pack(nat):
    at = lanes(8)
    out = []
    for h in range(2):
        acc = jnp.zeros((8, I), f32)
        for b in range(8):
            shift = (12 * b - 12 * h) % I
            block = nat[8 * b : 8 * b + 8]
            block = pltpu.roll(block, shift, 1) if shift else block
            acc = jnp.where((at >= 12 * b) & (at < 12 * b + 12), block, acc)
        out.append(acc)
    return out


def unpack(first, second):
    at = lanes(8)
    blocks = []
    for b in range(8):
        one = left(first, 12 * b)
        shift = (12 - 12 * b) % I
        two = pltpu.roll(second, shift, 1) if shift else second
        blocks.append(jnp.where(at < 12, one, jnp.where(at < 24, two, 0.0)))
    return jnp.concatenate(blocks, axis=0)


def kernel(
    x_hbm, er_hbm, sp_hbm, nr_hbm, vert_hbm, out_hbm,
    xin, er, sp, nr, vert, erp, win, suf, sl, sf, wb, gb, ob,
    s1, r1, s2, r2, s3, r3, s4, r4, in_sem, out_sem, send_sem, recv_sem,
):
    e = lax.axis_index("lon")
    q = lax.axis_index("lat")
    ve, vq = e // 8, q // 16

    loads = [
        pltpu.make_async_copy(sp_hbm, sp, in_sem.at[0]),
        pltpu.make_async_copy(er_hbm, er, in_sem.at[1]),
    ]
    for v in range(V):
        for b in range(3):
            n = 3 * v + b
            loads.append(
                pltpu.make_async_copy(x_hbm.at[v, :, pl.ds(8 * b, 8), :], xin.at[n], in_sem.at[2 + n])
            )
    loads.append(pltpu.make_async_copy(nr_hbm, nr, in_sem.at[8]))
    loads.append(pltpu.make_async_copy(vert_hbm, vert, in_sem.at[9]))
    for load in loads:
        load.start()

    barrier = pltpu.get_barrier_semaphore()

    @pl.loop(1, LON)
    def _(t):
        pl.semaphore_signal(barrier, inc=1, device_id={"lon": lax.rem(e + t, LON)}, device_id_type=MESH)

    @pl.loop(1, LAT)
    def _(t):
        pl.semaphore_signal(barrier, inc=1, device_id={"lat": lax.rem(q + t, LAT)}, device_id_type=MESH)

    loads[0].wait()
    spike = sp[...]
    at24 = lanes(J)
    window = jnp.where(at24 < I - 1, spike, 0.0)
    suffix = spike
    for k in range(7):
        win[k] = window
        step = 1 << k
        window = window * left(window, step)
        suffix = suffix * jnp.where(at24 < I - step, left(suffix, step), 1.0)
    suf[...] = suffix
    at1 = lanes(1)
    block_spike = jnp.zeros((1, I), f32)
    for j in range(J):
        block_spike = jnp.where(at1 == j, suffix[j : j + 1, 0:1], block_spike)

    loads[1].wait()
    erp[...] = jnp.zeros_like(erp)
    for v in range(V):
        erp[v, :, 0:J] = er[v]

    at64 = lanes(L)
    xflat = xin.reshape(V * 3 * L * 8, I)
    oflat = ob.reshape(V * 3 * L * 8, I)

    def scan_zonal(v):
        rate = erp[v]
        nat = jnp.zeros((L, I), f32)
        for j in range(J):
            if j % 8 == 0:
                loads[2 + 3 * v + j // 8].wait()
            x = xflat[pl.ds((3 * v + j // 8) * L * 8 + j % 8, L, stride=8), :]
            power = column(rate, j)
            for k in range(7):
                x = x + power * win[k, j : j + 1, :] * left(x, 1 << k)
                power = power * power
            sl[v, j] = x
            nat = jnp.where(at64 == j, pltpu.roll(x, j, 1) if j else x, nat)
        whole = rate
        for k in range(7):
            whole = whole * whole
        whole = whole * block_spike
        for h, part in enumerate(pack(nat)):
            for s in range(8):
                s1[8 * v + s, h : h + 1, :] = part[s : s + 1]
        for h, part in enumerate(pack(whole)):
            for s in range(8):
                s1[8 * v + s, 2 + h : 3 + h, :] = part[s : s + 1]

    def exchange(src, dst, axis, me, size, first, count, send, recv):
        @pl.loop(0, count)
        def _(t):
            to = first + lax.rem(me + t, count)

            @pl.when(to != me)
            def _():
                pltpu.make_async_remote_copy(
                    src_ref=src.at[to], dst_ref=dst.at[me], send_sem=send, recv_sem=recv,
                    device_id={axis: to}, device_id_type=MESH,
                ).start()

            @pl.when(to == me)
            def _():
                pltpu.make_async_copy(src.at[me], dst.at[me], recv).start()

    def wait(ref, first, count, sem):
        part = ref.at[pl.ds(first, count)]
        pltpu.make_async_copy(part, part, sem).wait()

    def scale_zonal(v):
        rate = erp[v]
        logs = jnp.maximum(jnp.log(rate) * 1.4426950408889634, -200.0)
        left_over = (I - at64).astype(f32)
        for j in range(J):
            a = column(rate, j) * sp[j : j + 1, :]
            s = root(1.0 - a * a)
            f = jnp.exp2(column(logs, j) * left_over) * suf[j : j + 1, :]
            sl[v, j] = s * sl[v, j]
            sf[v, j] = s * f

    scan_zonal(0)
    pl.semaphore_wait(barrier, LON + LAT - 2)
    exchange(s1, r1, "lon", e, LON, 0, 8, send_sem.at[0], recv_sem.at[0])
    scan_zonal(1)
    exchange(s1, r1, "lon", e, LON, 8, 8, send_sem.at[0], recv_sem.at[0])
    scale_zonal(0)
    scale_zonal(1)

    wait(r1, 0, LON, recv_sem.at[0])
    total = jnp.zeros((2, I), f32)
    around = jnp.ones((2, I), f32)
    for d in reversed(range(LON)):
        total = r1[d, 0:2, :] + r1[d, 2:4, :] * total
        around = around * r1[d, 2:4, :]
    carry = total / (1.0 - around)
    for d in reversed(range(LON)):
        s2[d] = carry
        carry = r1[d, 0:2, :] + r1[d, 2:4, :] * carry
    exchange(s2, r2, "lon", e, LON, 0, LON, send_sem.at[1], recv_sem.at[1 + ve])

    loads[8].wait()
    start = J * q
    tile, skip = start // I, lax.rem(start, I)
    back = lax.rem(I - skip, I)
    nxt = jnp.minimum(tile + 1, 5)
    north, scale, reach = [], [], []
    for v in range(V):
        one = pltpu.roll(nr[v, :, pl.ds(pl.multiple_of(tile * I, I), I)], back, 1)
        two = pltpu.roll(nr[v, :, pl.ds(pl.multiple_of(nxt * I, I), I)], back, 1)
        rates = jnp.where(at64 < I - skip, one, two)
        north.append(rates)
        s = root(1.0 - rates * rates)
        grown = rates
        for k in range(5):
            step = 1 << k
            grown = grown * jnp.where(at64 >= step, pltpu.roll(grown, step, 1), 1.0)
        scale.append(s)
        reach.append(s * grown)

    rows = nr[vq, pl.ds(pl.multiple_of(8 * (lax.rem(q, 16) // 2), 8), 8), :]
    two = rows * left(rows, 1)
    four = two * left(two, 2)
    eight = four * left(four, 4)
    sixteen = eight * left(eight, 8)
    band = sixteen * left(eight, 16)
    band = jnp.where(lax.rem(q, 2) == 0, band[0:4], band[4:8])
    for d in range(LAT):
        gb[d] = jnp.broadcast_to(band[:, J * d : J * d + 1], (4, I))

    loads[9].wait()
    mats = []
    for v in range(V):
        t = vert[v].T
        hi = t.astype(jnp.bfloat16)
        lo = (t - hi.astype(f32)).astype(jnp.bfloat16)
        mats.append(jnp.concatenate([hi, hi, lo], axis=1))

    def filter_north(v):
        wait(r2, 8 * v, 8, recv_sem.at[1 + v])
        halves = []
        for h in range(2):
            halves.append(jnp.concatenate([r2[8 * v + s, h : h + 1, :] for s in range(8)], axis=0))
        inc = unpack(*halves)
        w = jnp.zeros((L, I), f32)
        for j in range(J):
            w = sl[v, j] + sf[v, j] * column(inc, j) + column(north[v], j) * w
            wb[v, j] = w
        for b in range(16):
            s3[16 * v + b] = w[4 * b : 4 * b + 4]
        exchange(s3, r3, "lat", q, LAT, 16 * v, 16, send_sem.at[2], recv_sem.at[3])

    filter_north(0)
    filter_north(1)
    for v in range(V):
        for j in range(J):
            wb[v, j] = wb[v, j] * column(scale[v], j)

    wait(r3, 0, LAT, recv_sem.at[3])
    carry = jnp.zeros((4, I), f32)
    for d in range(LAT):
        s4[d] = carry
        carry = r3[d] + gb[d] * carry
    exchange(s4, r4, "lat", q, LAT, 0, LAT, send_sem.at[3], recv_sem.at[4 + vq])

    stores = []
    for v in range(V):
        wait(r4, 16 * v, 16, recv_sem.at[4 + v])
        carry = jnp.concatenate([r4[16 * v + b] for b in range(16)], axis=0)
        for j in range(0, J, 2):
            his, los = [], []
            for jj in (j, j + 1):
                m = wb[v, jj] + column(reach[v], jj) * carry
                hi = m.astype(jnp.bfloat16)
                his.append(hi)
                los.append((m - hi.astype(f32)).astype(jnp.bfloat16))
            hi = jnp.concatenate(his, axis=1)
            lo = jnp.concatenate(los, axis=1)
            y = jnp.dot(mats[v], jnp.concatenate([hi, lo, hi], axis=0), preferred_element_type=f32)
            for n, jj in enumerate((j, j + 1)):
                oflat[pl.ds((3 * v + jj // 8) * L * 8 + jj % 8, L, stride=8), :] = y[:, I * n : I * n + I]
            if j % 8 == 6:
                n = 3 * v + j // 8
                store = pltpu.make_async_copy(ob.at[n], out_hbm.at[v, :, pl.ds(8 * (j // 8), 8), :], out_sem.at[n])
                store.start()
                stores.append(store)
    wait(s1, 0, LON - 1, send_sem.at[0])
    wait(s2, 0, LON - 1, send_sem.at[1])
    wait(s3, 0, LAT - 1, send_sem.at[2])
    wait(s4, 0, LAT - 1, send_sem.at[3])
    for store in stores:
        store.wait()


def shards(increment, eastward_rate, eastward_spike, northward_rate, vertical):
    anywhere = pl.BlockSpec(memory_space=pl.ANY)
    vm = pltpu.VMEM
    return pl.pallas_call(
        kernel,
        out_shape=jax.ShapeDtypeStruct((V, L, J, I), f32),
        in_specs=[anywhere] * 5,
        out_specs=anywhere,
        scratch_shapes=[
            vm((V * 3, L, 8, I), f32),
            vm((V, L, J), f32),
            vm((J, I), f32),
            vm((V, L, J * LAT), f32),
            vm((V, L, L), f32),
            vm((V, L, I), f32),
            vm((7, J, I), f32),
            vm((J, I), f32),
            vm((V, J, L, I), f32),
            vm((V, J, L, I), f32),
            vm((V, J, L, I), f32),
            vm((LAT, 4, I), f32),
            vm((V * 3, L, 8, I), f32),
            vm((LON, 4, I), f32),
            vm((LON, 4, I), f32),
            vm((LON, 2, I), f32),
            vm((LON, 2, I), f32),
            vm((LAT, 4, I), f32),
            vm((LAT, 4, I), f32),
            vm((LAT, 4, I), f32),
            vm((LAT, 4, I), f32),
            pltpu.SemaphoreType.DMA((10,)),
            pltpu.SemaphoreType.DMA((6,)),
            pltpu.SemaphoreType.DMA((4,)),
            pltpu.SemaphoreType.DMA((6,)),
        ],
        compiler_params=pltpu.CompilerParams(
            collective_id=0, has_side_effects=True, vmem_limit_bytes=56 * 1024 * 1024
        ),
    )(increment, eastward_rate, eastward_spike, northward_rate, vertical)


def solution(mesh):
    return jax.shard_map(
        shards,
        mesh=mesh,
        in_specs=(P(None, None, "lat", "lon"), P(None, None, "lat"), P("lat", "lon"), P(), P()),
        out_specs=P(None, None, "lat", "lon"),
        check_vma=False,
    )
```

```python
import jax
import jax.numpy as jnp
from jax import lax
from jax.experimental import pallas as pl
from jax.experimental.pallas import tpu as pltpu
from jax.sharding import PartitionSpec as P

V, L, J, I = 2, 64, 24, 128
LON, LAT = 16, 32
MESH = pl.DeviceIdType.MESH
f32 = jnp.float32


def lanes(rows):
    return lax.broadcasted_iota(jnp.int32, (rows, I), 1)


def left(x, n):
    size = x.shape[1]
    return pltpu.roll(x, size - n, 1) if n else x


def root(x):
    return x * lax.rsqrt(jnp.maximum(x, 1e-30))


def column(x, j):
    return jnp.broadcast_to(x[:, j : j + 1], (x.shape[0], I))


def pack(nat):
    at = lanes(8)
    out = []
    for h in range(2):
        acc = jnp.zeros((8, I), f32)
        for b in range(8):
            shift = (12 * b - 12 * h) % I
            block = nat[8 * b : 8 * b + 8]
            block = pltpu.roll(block, shift, 1) if shift else block
            acc = jnp.where((at >= 12 * b) & (at < 12 * b + 12), block, acc)
        out.append(acc)
    return out


def unpack(first, second):
    at = lanes(8)
    blocks = []
    for b in range(8):
        one = left(first, 12 * b)
        shift = (12 - 12 * b) % I
        two = pltpu.roll(second, shift, 1) if shift else second
        blocks.append(jnp.where(at < 12, one, jnp.where(at < 24, two, 0.0)))
    return jnp.concatenate(blocks, axis=0)


def kernel(
    x_hbm, er_hbm, sp_hbm, nr_hbm, vert_hbm, wb, inflow, extent, mixing,
    xin, er, sp, nr, vert, erp, win, suf, sl, sf, nb, gb, part, power,
    spikes, ends, s3, r3, s4, r4, in_sem, send_sem, recv_sem,
):
    e = lax.axis_index("lon")
    q = lax.axis_index("lat")
    vq = q // 16

    loads = [
        pltpu.make_async_copy(sp_hbm, sp, in_sem.at[0]),
        pltpu.make_async_copy(er_hbm, er, in_sem.at[1]),
    ]
    for v in range(V):
        for b in range(3):
            n = 3 * v + b
            loads.append(
                pltpu.make_async_copy(x_hbm.at[v, :, pl.ds(8 * b, 8), :], xin.at[n], in_sem.at[2 + n])
            )
    loads.append(pltpu.make_async_copy(nr_hbm, nr, in_sem.at[8]))
    loads.append(pltpu.make_async_copy(vert_hbm, vert, in_sem.at[9]))
    for load in loads:
        load.start()

    barrier = pltpu.get_barrier_semaphore()

    @pl.loop(1, LAT)
    def _(t):
        pl.semaphore_signal(barrier, inc=1, device_id={"lat": lax.rem(q + t, LAT)}, device_id_type=MESH)

    @pl.loop(1, LON)
    def _(t):
        pl.semaphore_signal(barrier, inc=1, device_id={"lon": lax.rem(e + t, LON)}, device_id_type=MESH)

    loads[0].wait()
    spike = sp[...]
    at24 = lanes(J)
    window = jnp.where(at24 < I - 1, spike, 0.0)
    suffix = spike
    for k in range(7):
        win[k] = window
        step = 1 << k
        window = window * left(window, step)
        suffix = suffix * jnp.where(at24 < I - step, left(suffix, step), 1.0)
    suf[...] = suffix
    at1 = lanes(1)
    for h in range(2):
        row = jnp.zeros((1, I), f32)
        for j in range(12):
            own = (lax.rem(at1, 12) == j) & (at1 < 96)
            row = jnp.where(own, suffix[12 * h + j : 12 * h + j + 1, 0:1], row)
        spikes[e, h : h + 1, :] = row

    loads[1].wait()
    erp[...] = jnp.zeros_like(erp)
    for v in range(V):
        erp[v, :, 0:J] = er[v].T

    at64 = lanes(L)
    left_over = (I - at64).astype(f32)
    xflat = xin.reshape(V * 3 * L * 8, I)

    def scan_zonal(v):
        def rows(b, nat):
            n = 3 * v + b
            pltpu.make_async_copy(x_hbm.at[v, :, pl.ds(8 * b, 8), :], xin.at[n], in_sem.at[2 + n]).wait()
            rate = pltpu.roll(erp[v], lax.rem(I - 8 * b, I), 1)
            for k in range(7):
                for jj in range(8):
                    if k == 0:
                        x = xflat[pl.ds(n * L * 8 + jj, L, stride=8), :]
                        p = column(rate, jj)
                    else:
                        x = part[jj]
                        p = power[jj]
                        p = p * p
                    x = x + p * win[k, pl.ds(8 * b + jj, 1), :] * left(x, 1 << k)
                    if k < 6:
                        power[jj] = p
                        part[jj] = x
                    else:
                        sl[v, 8 * b + jj] = x
                        nat = jnp.where(at64 == 8 * b + jj, jnp.broadcast_to(x[:, 0:1], (L, I)), nat)
            return nat

        nat = lax.fori_loop(0, 3, rows, jnp.zeros((L, I), f32))
        for h, tile in enumerate(pack(nat)):
            ends[e, v, h] = tile

    def spread(ref, of, send, recv):
        @pl.loop(1, LON)
        def _(t):
            mine = of(ref.at[e])
            pltpu.make_async_remote_copy(
                src_ref=mine, dst_ref=mine, send_sem=send, recv_sem=recv,
                device_id={"lon": lax.rem(e + t, LON)}, device_id_type=MESH,
            ).start()

    def exchange(src, dst, axis, me, size, first, count, send, recv):
        @pl.loop(0, count)
        def _(t):
            to = first + lax.rem(me + t, count)

            @pl.when(to != me)
            def _():
                pltpu.make_async_remote_copy(
                    src_ref=src.at[to], dst_ref=dst.at[me], send_sem=send, recv_sem=recv,
                    device_id={axis: to}, device_id_type=MESH,
                ).start()

            @pl.when(to == me)
            def _():
                pltpu.make_async_copy(src.at[me], dst.at[me], recv).start()

    def wait(ref, sem):
        pltpu.make_async_copy(ref, ref, sem).wait()

    scan_zonal(0)
    pl.semaphore_wait(barrier, LON + LAT - 2)
    spread(ends, lambda r: r.at[0], send_sem.at[1], recv_sem.at[1])
    spread(spikes, lambda r: r, send_sem.at[0], recv_sem.at[0])
    scan_zonal(1)
    spread(ends, lambda r: r.at[1], send_sem.at[2], recv_sem.at[2])

    loads[8].wait()
    start = J * q
    tile, skip = start // I, lax.rem(start, I)
    back = lax.rem(I - skip, I)
    nxt = jnp.minimum(tile + 1, 5)
    north, scale, reach, onward = [], [], [], []
    for v in range(V):
        one = pltpu.roll(nr[v, :, pl.ds(pl.multiple_of(tile * I, I), I)], back, 1)
        two = pltpu.roll(nr[v, :, pl.ds(pl.multiple_of(nxt * I, I), I)], back, 1)
        rates = jnp.where(at64 < I - skip, one, two)
        north.append(rates)
        s = root(1.0 - rates * rates)
        grown = rates
        for k in range(5):
            step = 1 << k
            grown = grown * jnp.where(at64 >= step, pltpu.roll(grown, step, 1), 1.0)
        scale.append(s)
        reach.append(s * grown)
        after = jnp.where(at64 < J - 1, left(rates, 1), 1.0)
        for k in range(5):
            after = after * left(after, 1 << k)
        onward.append(after)

    early = []
    for v in range(V):
        rate = erp[v]
        logs = jnp.maximum(jnp.log(rate) * 1.4426950408889634, -200.0)
        acc = jnp.zeros((L, I), f32)
        for j in range(J):
            a = column(rate, j) * sp[j : j + 1, :]
            s = root(1.0 - a * a)
            f = jnp.exp2(column(logs, j) * left_over) * suf[j : j + 1, :]
            x = s * sl[v, j]
            n = column(north[v], j)
            sl[v, j] = x
            sf[v, j] = s * f
            nb[v, j] = n
            acc = x + n * acc
        early.append(acc)

    rows = nr[vq, pl.ds(pl.multiple_of(8 * (lax.rem(q, 16) // 2), 8), 8), :]
    two = rows * left(rows, 1)
    four = two * left(two, 2)
    eight = four * left(four, 4)
    sixteen = eight * left(eight, 8)
    band = sixteen * left(eight, 16)
    band = jnp.where(lax.rem(q, 2) == 0, band[0:4], band[4:8])
    for d in range(LAT):
        gb[d] = jnp.broadcast_to(band[:, J * d : J * d + 1], (4, I))

    loads[9].wait()
    for v in range(V):
        t = vert[v].T
        hi = t.astype(jnp.bfloat16)
        lo = (t - hi.astype(f32)).astype(jnp.bfloat16)
        mixing[v] = jnp.concatenate([hi, hi, lo], axis=1)
        extent[v] = reach[v]

    wholes = []
    for v in range(V):
        whole = erp[v]
        for k in range(7):
            whole = whole * whole
        wholes.append(pack(whole))

    incoming = []
    for v in range(V):
        if v == 0:
            wait(spikes.at[pl.ds(0, LON - 1)], recv_sem.at[0])
        wait(ends.at[pl.ds(0, LON - 1), v], recv_sem.at[1 + v])
        halves = []
        for h in range(2):
            total = jnp.zeros((8, I), f32)
            around = jnp.ones((8, I), f32)
            for d in reversed(range(1, LON + 1)):
                at = lax.rem(e + d, LON)
                factor = wholes[v][h] * spikes[at, h : h + 1, :]
                total = ends[at, v, h] + factor * total
                around = around * factor
            halves.append(total / (1.0 - around))
        inc = unpack(*halves)
        incoming.append(inc)
        push = inc * onward[v]
        acc = early[v]
        for j in range(J):
            acc = acc + sf[v, j] * column(push, j)
        for b in range(16):
            s3[16 * v + b] = acc[4 * b : 4 * b + 4]
        exchange(s3, r3, "lat", q, LAT, 16 * v, 16, send_sem.at[3], recv_sem.at[3])

    for v in range(V):
        w = jnp.zeros((L, I), f32)
        for j in range(J):
            w = sl[v, j] + sf[v, j] * column(incoming[v], j) + nb[v, j] * w
            wb[v, j] = w * column(scale[v], j)

    wait(r3, recv_sem.at[3])
    carry = jnp.zeros((4, I), f32)
    for d in range(LAT):
        s4[d] = carry
        carry = r3[d] + gb[d] * carry
    exchange(s4, r4, "lat", q, LAT, 0, LAT, send_sem.at[4], recv_sem.at[4 + vq])

    for v in range(V):
        wait(r4.at[pl.ds(16 * v, 16)], recv_sem.at[4 + v])
        for b in range(16):
            inflow[v, 4 * b : 4 * b + 4] = r4[16 * v + b]
    wait(spikes.at[pl.ds(0, LON - 1)], send_sem.at[0])
    wait(ends.at[pl.ds(0, LON - 1), 0], send_sem.at[1])
    wait(ends.at[pl.ds(0, LON - 1), 1], send_sem.at[2])
    wait(s3.at[pl.ds(0, LAT - 1)], send_sem.at[3])
    wait(s4.at[pl.ds(0, LAT - 1)], send_sem.at[4])


def finish(wb, inflow, extent, mixing, out_hbm, ob, out_sem):
    oflat = ob.reshape(V * 3 * L * 8, I)
    stores = []
    for v in range(V):
        carry = inflow[v]
        for j in range(0, J, 2):
            his, los = [], []
            for jj in (j, j + 1):
                m = wb[v, jj] + column(extent[v], jj) * carry
                hi = m.astype(jnp.bfloat16)
                his.append(hi)
                los.append((m - hi.astype(f32)).astype(jnp.bfloat16))
            hi = jnp.concatenate(his, axis=1)
            lo = jnp.concatenate(los, axis=1)
            y = jnp.dot(mixing[v], jnp.concatenate([hi, lo, hi], axis=0), preferred_element_type=f32)
            for n, jj in enumerate((j, j + 1)):
                oflat[pl.ds((3 * v + jj // 8) * L * 8 + jj % 8, L, stride=8), :] = y[:, I * n : I * n + I]
            if j % 8 == 6:
                n = 3 * v + j // 8
                store = pltpu.make_async_copy(ob.at[n], out_hbm.at[v, :, pl.ds(8 * (j // 8), 8), :], out_sem.at[n])
                store.start()
                stores.append(store)
    for store in stores:
        store.wait()


def shards(increment, eastward_rate, eastward_spike, northward_rate, vertical):
    anywhere = pl.BlockSpec(memory_space=pltpu.HBM)
    vm = pltpu.VMEM
    here = pl.BlockSpec(memory_space=pltpu.VMEM)
    held = [
        pltpu.with_memory_space_constraint(a, pltpu.HBM)
        for a in (increment, eastward_rate.transpose(0, 2, 1), eastward_spike, northward_rate, vertical)
    ]
    parts = pl.pallas_call(
        kernel,
        out_shape=[
            vm((V, J, L, I), f32),
            vm((V, L, I), f32),
            vm((V, L, I), f32),
            vm((V, L, 3 * L), jnp.bfloat16),
        ],
        in_specs=[anywhere] * 5,
        out_specs=[here] * 4,
        scratch_shapes=[
            vm((V * 3, L, 8, I), f32),
            vm((V, J, L), f32),
            vm((J, I), f32),
            vm((V, L, J * LAT), f32),
            vm((V, L, L), f32),
            vm((V, L, I), f32),
            vm((7, J, I), f32),
            vm((J, I), f32),
            vm((V, J, L, I), f32),
            vm((V, J, L, I), f32),
            vm((V, J, L, I), f32),
            vm((LAT, 4, I), f32),
            vm((8, L, I), f32),
            vm((8, L, I), f32),
            vm((LON, 2, I), f32),
            vm((LON, V, 2, 8, I), f32),
            vm((LAT, 4, I), f32),
            vm((LAT, 4, I), f32),
            vm((LAT, 4, I), f32),
            vm((LAT, 4, I), f32),
            pltpu.SemaphoreType.DMA((10,)),
            pltpu.SemaphoreType.DMA((5,)),
            pltpu.SemaphoreType.DMA((6,)),
        ],
        compiler_params=pltpu.CompilerParams(
            collective_id=0, has_side_effects=True, vmem_limit_bytes=48 * 1024 * 1024
        ),
    )(*held)
    return pl.pallas_call(
        finish,
        out_shape=jax.ShapeDtypeStruct((V, L, J, I), f32),
        in_specs=[here] * 4,
        out_specs=anywhere,
        scratch_shapes=[vm((V * 3, L, 8, I), f32), pltpu.SemaphoreType.DMA((6,))],
        compiler_params=pltpu.CompilerParams(vmem_limit_bytes=48 * 1024 * 1024),
    )(*parts)


def solution(mesh):
    return jax.shard_map(
        shards,
        mesh=mesh,
        in_specs=(P(None, None, "lat", "lon"), P(None, None, "lat"), P("lat", "lon"), P(), P()),
        out_specs=P(None, None, "lat", "lon"),
        check_vma=False,
    )
```

```python
import jax
import jax.numpy as jnp
from jax import lax
from jax.experimental import pallas as pl
from jax.experimental.pallas import tpu as pltpu
from jax.sharding import PartitionSpec as P

V, L, J, I = 2, 64, 24, 128
LON, LAT = 16, 32
MESH = pl.DeviceIdType.MESH
f32 = jnp.float32


def lanes(rows):
    return lax.broadcasted_iota(jnp.int32, (rows, I), 1)


def left(x, n):
    size = x.shape[1]
    return pltpu.roll(x, size - n, 1) if n else x


def root(x):
    return x * lax.rsqrt(jnp.maximum(x, 1e-30))


def column(x, j):
    return jnp.broadcast_to(x[:, j : j + 1], (x.shape[0], I))


def pack(nats):
    at = lanes(8)
    tiles = [jnp.zeros((8, I), f32)] * 3
    for v in range(V):
        for b in range(8):
            t, c = divmod(8 * J * v + J * b, I)
            block = nats[v][8 * b : 8 * b + 8]
            block = pltpu.roll(block, c, 1) if c else block
            tiles[t] = jnp.where((at >= c) & (at < c + J), block, tiles[t])
            if c + J > I:
                tiles[t + 1] = jnp.where(at < c + J - I, block, tiles[t + 1])
    return tiles


def unpack(tiles, v):
    at = lanes(8)
    blocks = []
    for b in range(8):
        t, c = divmod(8 * J * v + J * b, I)
        block = left(tiles[t], c)
        if c + J > I:
            block = jnp.where(at < I - c, block, left(tiles[t + 1], c))
        blocks.append(jnp.where(at < J, block, 0.0))
    return jnp.concatenate(blocks, axis=0)


def kernel(
    x_hbm, er_hbm, sp_hbm, nr_hbm, vert_hbm, wb, inflow, extent, mixing,
    xin, er, sp, nr, vert, erp, logs, win, pre, suf, sl, sf, nb, gb, part, power,
    scale, onward, early, whole_tiles, spikes, shares, ends, s3, r3, s4, r4, in_sem, send_sem, recv_sem,
):
    e = lax.axis_index("lon")
    q = lax.axis_index("lat")
    vq = q // 16

    loads = [
        pltpu.make_async_copy(sp_hbm, sp, in_sem.at[0]),
        pltpu.make_async_copy(er_hbm, er, in_sem.at[1]),
    ]
    for v in range(V):
        for b in range(3):
            n = 3 * v + b
            loads.append(
                pltpu.make_async_copy(x_hbm.at[v, :, pl.ds(8 * b, 8), :], xin.at[n], in_sem.at[2 + n])
            )
    loads.append(pltpu.make_async_copy(nr_hbm, nr, in_sem.at[8]))
    loads.append(pltpu.make_async_copy(vert_hbm, vert, in_sem.at[9]))
    for load in loads:
        load.start()

    barrier = pltpu.get_barrier_semaphore()

    for t in range(1, LAT):
        pl.semaphore_signal(barrier, inc=1, device_id={"lat": lax.rem(q + t, LAT)}, device_id_type=MESH)

    for t in range(1, LON):
        pl.semaphore_signal(barrier, inc=1, device_id={"lon": lax.rem(e + t, LON)}, device_id_type=MESH)

    loads[0].wait()
    spike = sp[...]
    at24 = lanes(J)
    prefix = jnp.where(at24 >= 1, pltpu.roll(spike, 1, 1), 1.0)
    for k in range(7):
        step = 1 << k
        prefix = prefix * jnp.where(at24 >= step, pltpu.roll(prefix, step, 1), 1.0)
    pre[...] = prefix
    prefix = prefix * spike
    at1 = lax.rem(lanes(1), J)
    row = jnp.zeros((1, I), f32)
    for j in range(J):
        row = jnp.where(at1 == j, prefix[j : j + 1, I - 1 : I], row)
    spikes[e] = row

    loads[1].wait()
    erp[...] = jnp.zeros_like(erp)
    for v in range(V):
        erp[v, :, 0:J] = er[v].T
    for v in range(V):
        logs[v] = jnp.maximum(jnp.log(erp[v]) * 1.4426950408889634, -200.0)

    at64 = lanes(L)
    left_over = (I - at64).astype(f32)
    xflat = xin.reshape(V * 3 * L * 8, I)

    ones = jnp.ones((2 * I, I), jnp.bfloat16)
    along = at64.astype(f32)

    def sum_zonal(v):
        def rows(b, nat):
            n = 3 * v + b
            pltpu.make_async_copy(x_hbm.at[v, :, pl.ds(8 * b, 8), :], xin.at[n], in_sem.at[2 + n]).wait()
            rate = pltpu.roll(logs[v], lax.rem(I - 8 * b, I), 1)
            for jj in range(8):
                x = xflat[pl.ds(n * L * 8 + jj, L, stride=8), :]
                y = x * jnp.exp2(column(rate, jj) * along) * pre[pl.ds(8 * b + jj, 1), :]
                hi = y.astype(jnp.bfloat16)
                lo = (y - hi.astype(f32)).astype(jnp.bfloat16)
                total = jnp.dot(jnp.concatenate([hi, lo], axis=1), ones, preferred_element_type=f32)
                nat = jnp.where(at64 == 8 * b + jj, total, nat)
            return nat

        return lax.fori_loop(0, 3, rows, jnp.zeros((L, I), f32))

    def scan_zonal(v):
        @pl.loop(0, 3)
        def _(b):
            n = 3 * v + b
            rate = pltpu.roll(erp[v], lax.rem(I - 8 * b, I), 1)
            for k in range(7):
                for jj in range(8):
                    if k == 0:
                        x = xflat[pl.ds(n * L * 8 + jj, L, stride=8), :]
                        p = column(rate, jj)
                    else:
                        x = part[jj]
                        p = power[jj]
                        p = p * p
                    x = x + p * win[k, pl.ds(8 * b + jj, 1), :] * left(x, 1 << k)
                    if k < 6:
                        power[jj] = p
                        part[jj] = x
                    else:
                        sl[v, 8 * b + jj] = x

    def spread(ref, send, recv):
        mine = ref.at[e]
        for t in range(LON - 1):
            to = t + (t >= e).astype(jnp.int32)
            pltpu.make_async_remote_copy(
                src_ref=mine, dst_ref=mine, send_sem=send, recv_sem=recv,
                device_id={"lon": to}, device_id_type=MESH,
            ).start()

    def exchange(src, dst, axis, me, size, first, count, send, recv):
        def send_one(t):
            to = first + lax.rem(me + t, count)
            pltpu.make_async_remote_copy(
                src_ref=src.at[to], dst_ref=dst.at[me], send_sem=send, recv_sem=recv,
                device_id={axis: to}, device_id_type=MESH,
            ).start()

        for t in range(1, count):
            send_one(t)
        mine = me // count == first // count

        @pl.when(mine)
        def _():
            pltpu.make_async_copy(src.at[me], dst.at[me], recv).start()

        @pl.when(jnp.logical_not(mine))
        def _():
            send_one(0)

    def wait(ref, sem):
        pltpu.make_async_copy(ref, ref, sem).wait()

    for t, tile in enumerate(pack([sum_zonal(0), sum_zonal(1)])):
        ends[e, t] = tile

    def prepare_first():
        window = jnp.where(at24 < I - 1, spike, 0.0)
        suffix = spike
        for k in range(7):
            win[k] = window
            step = 1 << k
            window = window * left(window, step)
            suffix = suffix * jnp.where(at24 < I - step, left(suffix, step), 1.0)
        suf[...] = suffix

        scan_zonal(0)

    def prepare_second():
        scan_zonal(1)
        loads[8].wait()
        start = J * q
        tile, skip = start // I, lax.rem(start, I)
        back = lax.rem(I - skip, I)
        nxt = jnp.minimum(tile + 1, 5)
        north = []
        for v in range(V):
            one = pltpu.roll(nr[v, :, pl.ds(pl.multiple_of(tile * I, I), I)], back, 1)
            two = pltpu.roll(nr[v, :, pl.ds(pl.multiple_of(nxt * I, I), I)], back, 1)
            rates = jnp.where(at64 < I - skip, one, two)
            north.append(rates)
            s = root(1.0 - rates * rates)
            grown = rates
            for k in range(5):
                step = 1 << k
                grown = grown * jnp.where(at64 >= step, pltpu.roll(grown, step, 1), 1.0)
            scale[v] = s
            extent[v] = s * grown
            after = jnp.where(at64 < J - 1, left(rates, 1), 1.0)
            for k in range(5):
                after = after * left(after, 1 << k)
            onward[v] = after

        for v in range(V):
            rate = erp[v]
            acc = jnp.zeros((L, I), f32)
            for j in range(J):
                a = column(rate, j) * sp[j : j + 1, :]
                s = root(1.0 - a * a)
                f = jnp.exp2(column(logs[v], j) * left_over) * suf[j : j + 1, :]
                x = s * sl[v, j]
                n = column(north[v], j)
                sl[v, j] = x
                sf[v, j] = s * f
                nb[v, j] = n
                acc = x + n * acc
            early[v] = acc

        rows = nr[vq, pl.ds(pl.multiple_of(8 * (lax.rem(q, 16) // 2), 8), 8), :]
        two = rows * left(rows, 1)
        four = two * left(two, 2)
        eight = four * left(four, 4)
        sixteen = eight * left(eight, 8)
        band = sixteen * left(eight, 16)
        band = jnp.where(lax.rem(q, 2) == 0, band[0:4], band[4:8])
        for d in range(LAT):
            gb[d] = jnp.broadcast_to(band[:, J * d : J * d + 1], (4, I))

        loads[9].wait()
        for v in range(V):
            t = vert[v].T
            hi = t.astype(jnp.bfloat16)
            lo = (t - hi.astype(f32)).astype(jnp.bfloat16)
            mixing[v] = jnp.concatenate([hi, hi, lo], axis=1)

        wholes = []
        for v in range(V):
            whole = erp[v]
            for k in range(7):
                whole = whole * whole
            wholes.append(whole)
        for t, tile in enumerate(pack(wholes)):
            whole_tiles[t] = tile

    def open_and_send():
        pl.semaphore_wait(barrier, LON + LAT - 2)
        spread(spikes, send_sem.at[0], recv_sem.at[0])
        spread(ends, send_sem.at[1], recv_sem.at[1])

    @pl.loop(0, 2)
    def _(phase):
        @pl.when(phase == (e >= 8).astype(jnp.int32))
        def _():
            prepare_first()

        @pl.when(phase == (e >= 4).astype(jnp.int32))
        def _():
            prepare_second()

        @pl.when(phase == 0)
        def _():
            open_and_send()

    wait(spikes.at[pl.ds(0, LON - 1)], recv_sem.at[0])
    at16 = lanes(LON)
    share = jnp.concatenate([spikes[d] for d in range(LON)], axis=0)
    shares[0] = share
    shares[1] = jnp.where(at16 < I - 8, left(share, 8), pltpu.roll(share, 16, 1))
    shares[2] = jnp.where(at16 < I - 16, left(share, 16), pltpu.roll(share, 8, 1))
    wait(ends.at[pl.ds(0, LON - 1)], recv_sem.at[1])
    tiles = []
    for t in range(3):
        total = jnp.zeros((8, I), f32)
        around = jnp.ones((8, I), f32)
        for d in reversed(range(1, LON + 1)):
            at = lax.rem(e + d, LON)
            factor = whole_tiles[t] * shares[t, pl.ds(at, 1), :]
            total = ends[at, t] + factor * total
            around = around * factor
        tiles.append(total / (1.0 - around))
    incoming = []
    for v in range(V):
        inc = unpack(tiles, v)
        incoming.append(inc)
        push = inc * onward[v]
        acc = early[v]
        for j in range(J):
            acc = acc + sf[v, j] * column(push, j)
        for b in range(16):
            s3[16 * v + b] = acc[4 * b : 4 * b + 4]
        exchange(s3, r3, "lat", q, LAT, 16 * v, 16, send_sem.at[3], recv_sem.at[3])

    for v in range(V):
        w = jnp.zeros((L, I), f32)
        for j in range(J):
            w = sl[v, j] + sf[v, j] * column(incoming[v], j) + nb[v, j] * w
            wb[v, j] = w * column(scale[v], j)

    wait(r3, recv_sem.at[3])
    carry = jnp.zeros((4, I), f32)
    for d in range(LAT):
        s4[d] = carry
        carry = r3[d] + gb[d] * carry
    pltpu.make_async_copy(s4.at[q], r4.at[q], recv_sem.at[4 + vq]).start()
    for t in range(LAT - 1):
        to = t + (t >= q).astype(jnp.int32)
        pltpu.make_async_remote_copy(
            src_ref=s4.at[to], dst_ref=r4.at[q], send_sem=send_sem.at[4], recv_sem=recv_sem.at[4 + vq],
            device_id={"lat": to}, device_id_type=MESH,
        ).start()

    for v in range(V):
        wait(r4.at[pl.ds(16 * v, 16)], recv_sem.at[4 + v])
        for b in range(16):
            inflow[v, 4 * b : 4 * b + 4] = r4[16 * v + b]
    wait(spikes.at[pl.ds(0, LON - 1)], send_sem.at[0])
    wait(ends.at[pl.ds(0, LON - 1)], send_sem.at[1])
    wait(s3.at[pl.ds(0, LAT - 1)], send_sem.at[3])
    wait(s4.at[pl.ds(0, LAT - 1)], send_sem.at[4])


def finish(wb, inflow, extent, mixing, out_hbm, ob, out_sem):
    oflat = ob.reshape(V * 3 * L * 8, I)
    stores = []
    for v in range(V):
        carry = inflow[v]
        for j in range(0, J, 2):
            his, los = [], []
            for jj in (j, j + 1):
                m = wb[v, jj] + column(extent[v], jj) * carry
                hi = m.astype(jnp.bfloat16)
                his.append(hi)
                los.append((m - hi.astype(f32)).astype(jnp.bfloat16))
            hi = jnp.concatenate(his, axis=1)
            lo = jnp.concatenate(los, axis=1)
            y = jnp.dot(mixing[v], jnp.concatenate([hi, lo, hi], axis=0), preferred_element_type=f32)
            for n, jj in enumerate((j, j + 1)):
                oflat[pl.ds((3 * v + jj // 8) * L * 8 + jj % 8, L, stride=8), :] = y[:, I * n : I * n + I]
            if j % 8 == 6:
                n = 3 * v + j // 8
                store = pltpu.make_async_copy(ob.at[n], out_hbm.at[v, :, pl.ds(8 * (j // 8), 8), :], out_sem.at[n])
                store.start()
                stores.append(store)
    for store in stores:
        store.wait()


def shards(increment, eastward_rate, eastward_spike, northward_rate, vertical):
    anywhere = pl.BlockSpec(memory_space=pltpu.HBM)
    vm = pltpu.VMEM
    here = pl.BlockSpec(memory_space=pltpu.VMEM)
    held = [
        pltpu.with_memory_space_constraint(a, pltpu.HBM)
        for a in (increment, eastward_rate.transpose(0, 2, 1), eastward_spike, northward_rate, vertical)
    ]
    parts = pl.pallas_call(
        kernel,
        out_shape=[
            vm((V, J, L, I), f32),
            vm((V, L, I), f32),
            vm((V, L, I), f32),
            vm((V, L, 3 * L), jnp.bfloat16),
        ],
        in_specs=[anywhere] * 5,
        out_specs=[here] * 4,
        scratch_shapes=[
            vm((V * 3, L, 8, I), f32),
            vm((V, J, L), f32),
            vm((J, I), f32),
            vm((V, L, J * LAT), f32),
            vm((V, L, L), f32),
            vm((V, L, I), f32),
            vm((V, L, I), f32),
            vm((7, J, I), f32),
            vm((J, I), f32),
            vm((J, I), f32),
            vm((V, J, L, I), f32),
            vm((V, J, L, I), f32),
            vm((V, J, L, I), f32),
            vm((LAT, 4, I), f32),
            vm((8, L, I), f32),
            vm((8, L, I), f32),
            vm((V, L, I), f32),
            vm((V, L, I), f32),
            vm((V, L, I), f32),
            vm((3, 8, I), f32),
            vm((LON, 1, I), f32),
            vm((3, LON, I), f32),
            vm((LON, 3, 8, I), f32),
            vm((LAT, 4, I), f32),
            vm((LAT, 4, I), f32),
            vm((LAT, 4, I), f32),
            vm((LAT, 4, I), f32),
            pltpu.SemaphoreType.DMA((10,)),
            pltpu.SemaphoreType.DMA((5,)),
            pltpu.SemaphoreType.DMA((6,)),
        ],
        compiler_params=pltpu.CompilerParams(
            collective_id=0, has_side_effects=True, vmem_limit_bytes=48 * 1024 * 1024
        ),
    )(*held)
    return pl.pallas_call(
        finish,
        out_shape=jax.ShapeDtypeStruct((V, L, J, I), f32),
        in_specs=[here] * 4,
        out_specs=anywhere,
        scratch_shapes=[vm((V * 3, L, 8, I), f32), pltpu.SemaphoreType.DMA((6,))],
        compiler_params=pltpu.CompilerParams(vmem_limit_bytes=48 * 1024 * 1024),
    )(*parts)


def solution(mesh):
    return jax.shard_map(
        shards,
        mesh=mesh,
        in_specs=(P(None, None, "lat", "lon"), P(None, None, "lat"), P("lat", "lon"), P(), P()),
        out_specs=P(None, None, "lat", "lon"),
        check_vma=False,
    )
```

```python
import jax
import jax.numpy as jnp
from jax import lax
from jax.experimental import pallas as pl
from jax.experimental.pallas import tpu as pltpu
from jax.sharding import PartitionSpec as P

V, L, J, I = 2, 64, 24, 128
Q = V * L // 4
LON, LAT = 16, 32
ROW, ROWS = 4, 8
MESH = pl.DeviceIdType.MESH
f32 = jnp.float32


def lanes(rows):
    return lax.broadcasted_iota(jnp.int32, (rows, I), 1)


def left(x, n):
    size = x.shape[1]
    return pltpu.roll(x, size - n, 1) if n else x


def root(x):
    return x * lax.rsqrt(jnp.maximum(x, 1e-30))


def column(x, j):
    return jnp.broadcast_to(x[:, j : j + 1], (x.shape[0], I))


def pack(nats):
    at = lanes(8)
    tiles = [jnp.zeros((8, I), f32)] * 3
    for v in range(V):
        for b in range(8):
            t, c = divmod(8 * J * v + J * b, I)
            block = nats[v][8 * b : 8 * b + 8]
            block = pltpu.roll(block, c, 1) if c else block
            tiles[t] = jnp.where((at >= c) & (at < c + J), block, tiles[t])
            if c + J > I:
                tiles[t + 1] = jnp.where(at < c + J - I, block, tiles[t + 1])
    return tiles


def unpack(tiles, v):
    at = lanes(8)
    blocks = []
    for b in range(8):
        t, c = divmod(8 * J * v + J * b, I)
        block = left(tiles[t], c)
        if c + J > I:
            block = jnp.where(at < I - c, block, left(tiles[t + 1], c))
        blocks.append(jnp.where(at < J, block, 0.0))
    return jnp.concatenate(blocks, axis=0)


def kernel(
    x_hbm, er_hbm, sp_hbm, nr_hbm, vert_hbm, wb, inflow, extent, mixing,
    xin, er, sp, nr, vert, erp, logs, win, pre, suf, sl, sf, nb, gb, gt, part, power,
    scale, onward, early, whole_tiles, spikes, shares, ends, s3, r3, st, rt, inside, s4, r4,
    in_sem, send_sem, recv_sem, row_send, row_recv,
):
    e = lax.axis_index("lon")
    q = lax.axis_index("lat")
    row, col = q // ROW, lax.rem(q, ROW)

    loads = [
        pltpu.make_async_copy(sp_hbm, sp, in_sem.at[0]),
        pltpu.make_async_copy(er_hbm, er, in_sem.at[1]),
    ]
    for v in range(V):
        for b in range(3):
            n = 3 * v + b
            loads.append(
                pltpu.make_async_copy(x_hbm.at[v, :, pl.ds(8 * b, 8), :], xin.at[n], in_sem.at[2 + n])
            )
    loads.append(pltpu.make_async_copy(nr_hbm, nr, in_sem.at[8]))
    loads.append(pltpu.make_async_copy(vert_hbm, vert, in_sem.at[9]))
    for load in loads:
        load.start()

    barrier = pltpu.get_barrier_semaphore()

    for t in range(1, LON):
        to = lax.rem(e + t, LON)
        pl.semaphore_signal(barrier, inc=1, device_id={"lon": to}, device_id_type=MESH)
    for t in range(1, ROWS):
        to = lax.rem(row + t, ROWS) * ROW + col
        pl.semaphore_signal(barrier, inc=1, device_id={"lat": to}, device_id_type=MESH)
    for t in range(1, ROW):
        to = row * ROW + lax.rem(col + t, ROW)
        pl.semaphore_signal(barrier, inc=1, device_id={"lat": to}, device_id_type=MESH)

    loads[0].wait()
    spike = sp[...]
    at24 = lanes(J)
    prefix = jnp.where(at24 >= 1, pltpu.roll(spike, 1, 1), 1.0)
    for k in range(7):
        step = 1 << k
        prefix = prefix * jnp.where(at24 >= step, pltpu.roll(prefix, step, 1), 1.0)
    pre[...] = prefix
    prefix = prefix * spike
    at1 = lax.rem(lanes(1), J)
    periodic = jnp.zeros((1, I), f32)
    for j in range(J):
        periodic = jnp.where(at1 == j, prefix[j : j + 1, I - 1 : I], periodic)
    spikes[e] = periodic

    loads[1].wait()
    erp[...] = jnp.zeros_like(erp)
    for v in range(V):
        erp[v, :, 0:J] = er[v].T
    for v in range(V):
        logs[v] = jnp.maximum(jnp.log(erp[v]) * 1.4426950408889634, -200.0)

    at64 = lanes(L)
    left_over = (I - at64).astype(f32)
    xflat = xin.reshape(V * 3 * L * 8, I)

    ones = jnp.ones((2 * I, I), jnp.bfloat16)
    along = at64.astype(f32)

    def sum_zonal(v):
        def rows(b, nat):
            n = 3 * v + b
            pltpu.make_async_copy(x_hbm.at[v, :, pl.ds(8 * b, 8), :], xin.at[n], in_sem.at[2 + n]).wait()
            rate = pltpu.roll(logs[v], lax.rem(I - 8 * b, I), 1)
            for jj in range(8):
                x = xflat[pl.ds(n * L * 8 + jj, L, stride=8), :]
                y = x * jnp.exp2(column(rate, jj) * along) * pre[pl.ds(8 * b + jj, 1), :]
                hi = y.astype(jnp.bfloat16)
                lo = (y - hi.astype(f32)).astype(jnp.bfloat16)
                total = jnp.dot(jnp.concatenate([hi, lo], axis=1), ones, preferred_element_type=f32)
                nat = jnp.where(at64 == 8 * b + jj, total, nat)
            return nat

        return lax.fori_loop(0, 3, rows, jnp.zeros((L, I), f32))

    def scan_zonal(v):
        @pl.loop(0, 3)
        def _(b):
            n = 3 * v + b
            rate = pltpu.roll(erp[v], lax.rem(I - 8 * b, I), 1)
            for k in range(7):
                for jj in range(8):
                    if k == 0:
                        x = xflat[pl.ds(n * L * 8 + jj, L, stride=8), :]
                        p = column(rate, jj)
                    else:
                        x = part[jj]
                        p = power[jj]
                        p = p * p
                    x = x + p * win[k, pl.ds(8 * b + jj, 1), :] * left(x, 1 << k)
                    if k < 6:
                        power[jj] = p
                        part[jj] = x
                    else:
                        sl[v, 8 * b + jj] = x

    def spread(ref, send, recv):
        mine = ref.at[e]
        for t in range(LON - 1):
            to = t + (t >= e).astype(jnp.int32)
            pltpu.make_async_remote_copy(
                src_ref=mine, dst_ref=mine, send_sem=send, recv_sem=recv,
                device_id={"lon": to}, device_id_type=MESH,
            ).start()

    def along_row(src, dst, quarter, to, send, recv):
        @pl.when(to == col)
        def _():
            pltpu.make_async_copy(src.at[quarter], dst.at[col], recv).start()

        @pl.when(to != col)
        def _():
            pltpu.make_async_remote_copy(
                src_ref=src.at[quarter], dst_ref=dst.at[col], send_sem=send, recv_sem=recv,
                device_id={"lat": row * ROW + to}, device_id_type=MESH,
            ).start()

    def wait(ref, sem):
        pltpu.make_async_copy(ref, ref, sem).wait()

    for t, tile in enumerate(pack([sum_zonal(0), sum_zonal(1)])):
        ends[e, t] = tile

    def prepare_first():
        window = jnp.where(at24 < I - 1, spike, 0.0)
        suffix = spike
        for k in range(7):
            win[k] = window
            step = 1 << k
            window = window * left(window, step)
            suffix = suffix * jnp.where(at24 < I - step, left(suffix, step), 1.0)
        suf[...] = suffix

        scan_zonal(0)

    def prepare_second():
        scan_zonal(1)
        loads[8].wait()
        start = J * q
        tile, skip = start // I, lax.rem(start, I)
        back = lax.rem(I - skip, I)
        nxt = jnp.minimum(tile + 1, 5)
        north = []
        for v in range(V):
            one = pltpu.roll(nr[v, :, pl.ds(pl.multiple_of(tile * I, I), I)], back, 1)
            two = pltpu.roll(nr[v, :, pl.ds(pl.multiple_of(nxt * I, I), I)], back, 1)
            rates = jnp.where(at64 < I - skip, one, two)
            north.append(rates)
            s = root(1.0 - rates * rates)
            grown = rates
            for k in range(5):
                step = 1 << k
                grown = grown * jnp.where(at64 >= step, pltpu.roll(grown, step, 1), 1.0)
            scale[v] = s
            extent[v] = s * grown
            after = jnp.where(at64 < J - 1, left(rates, 1), 1.0)
            for k in range(5):
                after = after * left(after, 1 << k)
            onward[v] = after

        for v in range(V):
            rate = erp[v]
            acc = jnp.zeros((L, I), f32)
            for j in range(J):
                a = column(rate, j) * sp[j : j + 1, :]
                s = root(1.0 - a * a)
                f = jnp.exp2(column(logs[v], j) * left_over) * suf[j : j + 1, :]
                x = s * sl[v, j]
                n = column(north[v], j)
                sl[v, j] = x
                sf[v, j] = s * f
                nb[v, j] = n
                acc = x + n * acc
            early[v] = acc

        rows = nr[col // 2, pl.ds(pl.multiple_of(Q * lax.rem(col, 2), Q), Q), :]
        two = rows * left(rows, 1)
        four = two * left(two, 2)
        eight = four * left(four, 4)
        sixteen = eight * left(eight, 8)
        band = sixteen * left(eight, 16)
        for r in range(ROWS):
            whole = jnp.ones((Q, I), f32)
            for c in range(ROW):
                d = ROW * r + c
                g = jnp.broadcast_to(band[:, J * d : J * d + 1], (Q, I))
                gb[d] = g
                whole = whole * g
            gt[r] = whole

        loads[9].wait()
        for v in range(V):
            t = vert[v].T
            hi = t.astype(jnp.bfloat16)
            lo = (t - hi.astype(f32)).astype(jnp.bfloat16)
            mixing[v] = jnp.concatenate([hi, hi, lo], axis=1)

        wholes = []
        for v in range(V):
            whole = erp[v]
            for k in range(7):
                whole = whole * whole
            wholes.append(whole)
        for t, tile in enumerate(pack(wholes)):
            whole_tiles[t] = tile

    def open_and_send():
        pl.semaphore_wait(barrier, LON + ROWS + ROW - 3)
        spread(spikes, send_sem.at[0], recv_sem.at[0])
        spread(ends, send_sem.at[1], recv_sem.at[1])

    @pl.loop(0, 2)
    def _(phase):
        @pl.when(phase == (e >= 8).astype(jnp.int32))
        def _():
            prepare_first()

        @pl.when(phase == (e >= 4).astype(jnp.int32))
        def _():
            prepare_second()

        @pl.when(phase == 0)
        def _():
            open_and_send()

    wait(spikes.at[pl.ds(0, LON - 1)], recv_sem.at[0])
    at16 = lanes(LON)
    share = jnp.concatenate([spikes[d] for d in range(LON)], axis=0)
    shares[0] = share
    shares[1] = jnp.where(at16 < I - 8, left(share, 8), pltpu.roll(share, 16, 1))
    shares[2] = jnp.where(at16 < I - 16, left(share, 16), pltpu.roll(share, 8, 1))
    wait(ends.at[pl.ds(0, LON - 1)], recv_sem.at[1])
    tiles = []
    for t in range(3):
        total = jnp.zeros((8, I), f32)
        around = jnp.ones((8, I), f32)
        for d in reversed(range(1, LON + 1)):
            at = lax.rem(e + d, LON)
            factor = whole_tiles[t] * shares[t, pl.ds(at, 1), :]
            total = ends[at, t] + factor * total
            around = around * factor
        tiles.append(total / (1.0 - around))
    incoming = []
    for v in range(V):
        inc = unpack(tiles, v)
        incoming.append(inc)
        push = inc * onward[v]
        acc = early[v]
        for j in range(J):
            acc = acc + sf[v, j] * column(push, j)
        for h in range(2):
            s3[2 * v + h] = acc[Q * h : Q * h + Q]
            along_row(s3, r3, 2 * v + h, 2 * v + h, send_sem.at[2], recv_sem.at[2])

    wait(r3, recv_sem.at[2])
    total = r3[0]
    for c in range(1, ROW):
        total = r3[c] + gb[ROW * row + c] * total
    st[...] = total
    for t in range(1, ROWS):

        @pl.when(row + t < ROWS)
        def _():
            pltpu.make_async_remote_copy(
                src_ref=st, dst_ref=rt.at[row], send_sem=row_send.at[t], recv_sem=row_recv.at[row],
                device_id={"lat": (row + t) * ROW + col}, device_id_type=MESH,
            ).start()

    def recurse(v):
        w = jnp.zeros((L, I), f32)
        for j in range(J):
            w = sl[v, j] + sf[v, j] * column(incoming[v], j) + nb[v, j] * w
            wb[v, j] = w * column(scale[v], j)

    recurse(0)
    inside[...] = jnp.zeros_like(inside)
    for r in range(ROWS - 1):

        @pl.when(r < row)
        def _():
            pltpu.make_async_copy(rt.at[r], rt.at[r], row_recv.at[r]).wait()
            inside[...] = rt[r] + gt[r] * inside[...]

    carry = inside[...]
    for c in range(ROW):
        s4[c] = carry
        along_row(s4, r4, c, c, send_sem.at[3], recv_sem.at[3])
        if c + 1 < ROW:
            carry = r3[c] + gb[ROW * row + c] * carry
    recurse(1)
    wait(r4, recv_sem.at[3])
    for v in range(V):
        for h in range(2):
            inflow[v, Q * h : Q * h + Q] = r4[2 * v + h]
    for t in range(1, ROWS):

        @pl.when(row + t < ROWS)
        def _():
            pltpu.make_async_copy(st, st, row_send.at[t]).wait()

    wait(spikes.at[pl.ds(0, LON - 1)], send_sem.at[0])
    wait(ends.at[pl.ds(0, LON - 1)], send_sem.at[1])
    wait(s3.at[pl.ds(0, ROW - 1)], send_sem.at[2])
    wait(s4.at[pl.ds(0, ROW - 1)], send_sem.at[3])


def finish(wb, inflow, extent, mixing, out_hbm, ob, out_sem):
    oflat = ob.reshape(V * 3 * L * 8, I)
    stores = []
    for v in range(V):
        carry = inflow[v]
        for j in range(0, J, 2):
            his, los = [], []
            for jj in (j, j + 1):
                m = wb[v, jj] + column(extent[v], jj) * carry
                hi = m.astype(jnp.bfloat16)
                his.append(hi)
                los.append((m - hi.astype(f32)).astype(jnp.bfloat16))
            hi = jnp.concatenate(his, axis=1)
            lo = jnp.concatenate(los, axis=1)
            y = jnp.dot(mixing[v], jnp.concatenate([hi, lo, hi], axis=0), preferred_element_type=f32)
            for n, jj in enumerate((j, j + 1)):
                oflat[pl.ds((3 * v + jj // 8) * L * 8 + jj % 8, L, stride=8), :] = y[:, I * n : I * n + I]
            if j % 8 == 6:
                n = 3 * v + j // 8
                store = pltpu.make_async_copy(ob.at[n], out_hbm.at[v, :, pl.ds(8 * (j // 8), 8), :], out_sem.at[n])
                store.start()
                stores.append(store)
    for store in stores:
        store.wait()


def shards(increment, eastward_rate, eastward_spike, northward_rate, vertical):
    anywhere = pl.BlockSpec(memory_space=pltpu.HBM)
    vm = pltpu.VMEM
    here = pl.BlockSpec(memory_space=pltpu.VMEM)
    held = [
        pltpu.with_memory_space_constraint(a, pltpu.HBM)
        for a in (increment, eastward_rate.transpose(0, 2, 1), eastward_spike, northward_rate, vertical)
    ]
    parts = pl.pallas_call(
        kernel,
        out_shape=[
            vm((V, J, L, I), f32),
            vm((V, L, I), f32),
            vm((V, L, I), f32),
            vm((V, L, 3 * L), jnp.bfloat16),
        ],
        in_specs=[anywhere] * 5,
        out_specs=[here] * 4,
        scratch_shapes=[
            vm((V * 3, L, 8, I), f32),
            vm((V, J, L), f32),
            vm((J, I), f32),
            vm((V, L, J * LAT), f32),
            vm((V, L, L), f32),
            vm((V, L, I), f32),
            vm((V, L, I), f32),
            vm((7, J, I), f32),
            vm((J, I), f32),
            vm((J, I), f32),
            vm((V, J, L, I), f32),
            vm((V, J, L, I), f32),
            vm((V, J, L, I), f32),
            vm((LAT, Q, I), f32),
            vm((ROWS, Q, I), f32),
            vm((8, L, I), f32),
            vm((8, L, I), f32),
            vm((V, L, I), f32),
            vm((V, L, I), f32),
            vm((V, L, I), f32),
            vm((3, 8, I), f32),
            vm((LON, 1, I), f32),
            vm((3, LON, I), f32),
            vm((LON, 3, 8, I), f32),
            vm((ROW, Q, I), f32),
            vm((ROW, Q, I), f32),
            vm((Q, I), f32),
            vm((ROWS, Q, I), f32),
            vm((Q, I), f32),
            vm((ROW, Q, I), f32),
            vm((ROW, Q, I), f32),
            pltpu.SemaphoreType.DMA((10,)),
            pltpu.SemaphoreType.DMA((4,)),
            pltpu.SemaphoreType.DMA((4,)),
            pltpu.SemaphoreType.DMA((ROWS,)),
            pltpu.SemaphoreType.DMA((ROWS,)),
        ],
        compiler_params=pltpu.CompilerParams(
            collective_id=0, has_side_effects=True, vmem_limit_bytes=48 * 1024 * 1024
        ),
    )(*held)
    return pl.pallas_call(
        finish,
        out_shape=jax.ShapeDtypeStruct((V, L, J, I), f32),
        in_specs=[here] * 4,
        out_specs=anywhere,
        scratch_shapes=[vm((V * 3, L, 8, I), f32), pltpu.SemaphoreType.DMA((6,))],
        compiler_params=pltpu.CompilerParams(vmem_limit_bytes=48 * 1024 * 1024),
    )(*parts)


def solution(mesh):
    return jax.shard_map(
        shards,
        mesh=mesh,
        in_specs=(P(None, None, "lat", "lon"), P(None, None, "lat"), P("lat", "lon"), P(), P()),
        out_specs=P(None, None, "lat", "lon"),
        check_vma=False,
    )
```

```python
import jax
import jax.numpy as jnp
from jax import lax
from jax.experimental import pallas as pl
from jax.experimental.pallas import tpu as pltpu
from jax.sharding import PartitionSpec as P

V, L, J, I = 2, 64, 24, 128
Q = V * L // 4
LON, LAT = 16, 32
ROW, ROWS = 4, 8
MESH = pl.DeviceIdType.MESH
f32 = jnp.float32
FAR_ROWS = (4, 3, 5, 2, 6, 1, 7)


def lanes(rows):
    return lax.broadcasted_iota(jnp.int32, (rows, I), 1)


def left(x, n):
    size = x.shape[1]
    return pltpu.roll(x, size - n, 1) if n else x


def root(x):
    return x * lax.rsqrt(jnp.maximum(x, 1e-30))


def column(x, j):
    return jnp.broadcast_to(x[:, j : j + 1], (x.shape[0], I))


def pack(nats):
    at = lanes(8)
    tiles = [jnp.zeros((8, I), f32)] * 3
    for v in range(V):
        for b in range(8):
            t, c = divmod(8 * J * v + J * b, I)
            block = nats[v][8 * b : 8 * b + 8]
            block = pltpu.roll(block, c, 1) if c else block
            tiles[t] = jnp.where((at >= c) & (at < c + J), block, tiles[t])
            if c + J > I:
                tiles[t + 1] = jnp.where(at < c + J - I, block, tiles[t + 1])
    return tiles


def unpack(tiles, v):
    at = lanes(8)
    blocks = []
    for b in range(8):
        t, c = divmod(8 * J * v + J * b, I)
        block = left(tiles[t], c)
        if c + J > I:
            block = jnp.where(at < I - c, block, left(tiles[t + 1], c))
        blocks.append(jnp.where(at < J, block, 0.0))
    return jnp.concatenate(blocks, axis=0)


def kernel(
    x_hbm, er_hbm, sp_hbm, nr_hbm, vert_hbm, wb, inflow, extent, mixing,
    xin, er, sp, nr, vert, erp, logs, win, pre, suf, sl, sf, nb, gb, gt, part, power,
    scale, onward, early, whole_tiles, spikes, shares, ends, s3, r3, st, rt, inside, s4, r4,
    in_sem, send_sem, recv_sem, row_send, row_recv,
):
    e = lax.axis_index("lon")
    q = lax.axis_index("lat")
    row, col = q // ROW, lax.rem(q, ROW)

    loads = [
        pltpu.make_async_copy(sp_hbm, sp, in_sem.at[0]),
        pltpu.make_async_copy(er_hbm, er, in_sem.at[1]),
    ]
    for v in range(V):
        for b in range(3):
            n = 3 * v + b
            loads.append(
                pltpu.make_async_copy(x_hbm.at[v, :, pl.ds(8 * b, 8), :], xin.at[n], in_sem.at[2 + n])
            )
    loads.append(pltpu.make_async_copy(nr_hbm, nr, in_sem.at[8]))
    loads.append(pltpu.make_async_copy(vert_hbm, vert, in_sem.at[9]))
    for load in loads:
        load.start()

    barrier = pltpu.get_barrier_semaphore()

    for t in range(1, LON):
        to = lax.rem(e + t, LON)
        pl.semaphore_signal(barrier, inc=1, device_id={"lon": to}, device_id_type=MESH)
    for t in range(1, ROWS):
        to = lax.rem(row + t, ROWS) * ROW + col
        pl.semaphore_signal(barrier, inc=1, device_id={"lat": to}, device_id_type=MESH)
    for t in range(1, ROW):
        to = row * ROW + lax.rem(col + t, ROW)
        pl.semaphore_signal(barrier, inc=1, device_id={"lat": to}, device_id_type=MESH)

    loads[0].wait()
    spike = sp[...]
    at24 = lanes(J)
    prefix = jnp.where(at24 >= 1, pltpu.roll(spike, 1, 1), 1.0)
    for k in range(7):
        step = 1 << k
        prefix = prefix * jnp.where(at24 >= step, pltpu.roll(prefix, step, 1), 1.0)
    pre[...] = prefix
    prefix = prefix * spike
    at1 = lax.rem(lanes(1), J)
    periodic = jnp.zeros((1, I), f32)
    for j in range(J):
        periodic = jnp.where(at1 == j, prefix[j : j + 1, I - 1 : I], periodic)
    spikes[e] = periodic

    loads[1].wait()
    erp[...] = jnp.zeros_like(erp)
    for v in range(V):
        erp[v, :, 0:J] = er[v].T
    for v in range(V):
        logs[v] = jnp.maximum(jnp.log(erp[v]) * 1.4426950408889634, -200.0)

    at64 = lanes(L)
    left_over = (I - at64).astype(f32)
    xflat = xin.reshape(V * 3 * L * 8, I)

    ones = jnp.ones((2 * I, I), jnp.bfloat16)
    along = at64.astype(f32)

    def sum_zonal(v):
        def rows(b, nat):
            n = 3 * v + b
            pltpu.make_async_copy(x_hbm.at[v, :, pl.ds(8 * b, 8), :], xin.at[n], in_sem.at[2 + n]).wait()
            rate = pltpu.roll(logs[v], lax.rem(I - 8 * b, I), 1)
            for jj in range(8):
                x = xflat[pl.ds(n * L * 8 + jj, L, stride=8), :]
                y = x * jnp.exp2(column(rate, jj) * along) * pre[pl.ds(8 * b + jj, 1), :]
                hi = y.astype(jnp.bfloat16)
                lo = (y - hi.astype(f32)).astype(jnp.bfloat16)
                total = jnp.dot(jnp.concatenate([hi, lo], axis=1), ones, preferred_element_type=f32)
                nat = jnp.where(at64 == 8 * b + jj, total, nat)
            return nat

        return lax.fori_loop(0, 3, rows, jnp.zeros((L, I), f32))

    def scan_zonal(v):
        @pl.loop(0, 3)
        def _(b):
            n = 3 * v + b
            rate = pltpu.roll(erp[v], lax.rem(I - 8 * b, I), 1)
            for k in range(7):
                for jj in range(8):
                    if k == 0:
                        x = xflat[pl.ds(n * L * 8 + jj, L, stride=8), :]
                        p = column(rate, jj)
                    else:
                        x = part[jj]
                        p = power[jj]
                        p = p * p
                    x = x + p * win[k, pl.ds(8 * b + jj, 1), :] * left(x, 1 << k)
                    if k < 6:
                        power[jj] = p
                        part[jj] = x
                    else:
                        sl[v, 8 * b + jj] = x

    def spread(ref, send, recv):
        mine = ref.at[e]
        for t in range(LON - 1):
            to = t + (t >= e).astype(jnp.int32)
            pltpu.make_async_remote_copy(
                src_ref=mine, dst_ref=mine, send_sem=send, recv_sem=recv,
                device_id={"lon": to}, device_id_type=MESH,
            ).start()

    def along_row(src, dst, quarter, to, send, recv):
        @pl.when(to == col)
        def _():
            pltpu.make_async_copy(src.at[quarter], dst.at[col], recv).start()

        @pl.when(to != col)
        def _():
            pltpu.make_async_remote_copy(
                src_ref=src.at[quarter], dst_ref=dst.at[col], send_sem=send, recv_sem=recv,
                device_id={"lat": row * ROW + to}, device_id_type=MESH,
            ).start()

    def wait(ref, sem):
        pltpu.make_async_copy(ref, ref, sem).wait()

    for t, tile in enumerate(pack([sum_zonal(0), sum_zonal(1)])):
        ends[e, t] = tile

    def prepare_first():
        window = jnp.where(at24 < I - 1, spike, 0.0)
        suffix = spike
        for k in range(7):
            win[k] = window
            step = 1 << k
            window = window * left(window, step)
            suffix = suffix * jnp.where(at24 < I - step, left(suffix, step), 1.0)
        suf[...] = suffix

        scan_zonal(0)

    def prepare_second():
        scan_zonal(1)
        loads[8].wait()
        start = J * q
        tile, skip = start // I, lax.rem(start, I)
        back = lax.rem(I - skip, I)
        nxt = jnp.minimum(tile + 1, 5)
        north = []
        for v in range(V):
            one = pltpu.roll(nr[v, :, pl.ds(pl.multiple_of(tile * I, I), I)], back, 1)
            two = pltpu.roll(nr[v, :, pl.ds(pl.multiple_of(nxt * I, I), I)], back, 1)
            rates = jnp.where(at64 < I - skip, one, two)
            north.append(rates)
            s = root(1.0 - rates * rates)
            grown = rates
            for k in range(5):
                step = 1 << k
                grown = grown * jnp.where(at64 >= step, pltpu.roll(grown, step, 1), 1.0)
            scale[v] = s
            extent[v] = s * grown
            after = jnp.where(at64 < J - 1, left(rates, 1), 1.0)
            for k in range(5):
                after = after * left(after, 1 << k)
            onward[v] = after

        for v in range(V):
            rate = erp[v]
            acc = jnp.zeros((L, I), f32)
            for j in range(J):
                a = column(rate, j) * sp[j : j + 1, :]
                s = root(1.0 - a * a)
                f = jnp.exp2(column(logs[v], j) * left_over) * suf[j : j + 1, :]
                x = s * sl[v, j]
                n = column(north[v], j)
                sl[v, j] = x
                sf[v, j] = s * f
                nb[v, j] = n
                acc = x + n * acc
            early[v] = acc

        rows = nr[col // 2, pl.ds(pl.multiple_of(Q * lax.rem(col, 2), Q), Q), :]
        two = rows * left(rows, 1)
        four = two * left(two, 2)
        eight = four * left(four, 4)
        sixteen = eight * left(eight, 8)
        band = sixteen * left(eight, 16)
        for r in range(ROWS):
            whole = jnp.ones((Q, I), f32)
            for c in range(ROW):
                d = ROW * r + c
                g = jnp.broadcast_to(band[:, J * d : J * d + 1], (Q, I))
                gb[d] = g
                whole = whole * g
            gt[r] = whole

        loads[9].wait()
        for v in range(V):
            t = vert[v].T
            hi = t.astype(jnp.bfloat16)
            lo = (t - hi.astype(f32)).astype(jnp.bfloat16)
            mixing[v] = jnp.concatenate([hi, hi, lo], axis=1)

        wholes = []
        for v in range(V):
            whole = erp[v]
            for k in range(7):
                whole = whole * whole
            wholes.append(whole)
        for t, tile in enumerate(pack(wholes)):
            whole_tiles[t] = tile

    def open_and_send():
        pl.semaphore_wait(barrier, LON + ROWS + ROW - 3)
        spread(spikes, send_sem.at[0], recv_sem.at[0])
        spread(ends, send_sem.at[1], recv_sem.at[1])

    @pl.loop(0, 2)
    def _(phase):
        @pl.when(phase == (e >= 8).astype(jnp.int32))
        def _():
            prepare_first()

        @pl.when(phase == (e >= 4).astype(jnp.int32))
        def _():
            prepare_second()

        @pl.when(phase == 0)
        def _():
            open_and_send()

    wait(spikes.at[pl.ds(0, LON - 1)], recv_sem.at[0])
    at16 = lanes(LON)
    share = jnp.concatenate([spikes[d] for d in range(LON)], axis=0)
    shares[0] = share
    shares[1] = jnp.where(at16 < I - 8, left(share, 8), pltpu.roll(share, 16, 1))
    shares[2] = jnp.where(at16 < I - 16, left(share, 16), pltpu.roll(share, 8, 1))
    wait(ends.at[pl.ds(0, LON - 1)], recv_sem.at[1])
    tiles = []
    for t in range(3):
        total = jnp.zeros((8, I), f32)
        around = jnp.ones((8, I), f32)
        for d in reversed(range(1, LON + 1)):
            at = lax.rem(e + d, LON)
            factor = whole_tiles[t] * shares[t, pl.ds(at, 1), :]
            total = ends[at, t] + factor * total
            around = around * factor
        tiles.append(total / (1.0 - around))
    incoming = []
    for v in range(V):
        inc = unpack(tiles, v)
        incoming.append(inc)
        push = inc * onward[v]
        acc = early[v]
        for j in range(J):
            acc = acc + sf[v, j] * column(push, j)
        for h in range(2):
            s3[2 * v + h] = acc[Q * h : Q * h + Q]
            along_row(s3, r3, 2 * v + h, 2 * v + h, send_sem.at[2], recv_sem.at[2])

    wait(r3, recv_sem.at[2])
    total = r3[0]
    for c in range(1, ROW):
        total = r3[c] + gb[ROW * row + c] * total
    st[...] = total
    for t in FAR_ROWS:

        @pl.when(row + t < ROWS)
        def _():
            pltpu.make_async_remote_copy(
                src_ref=st, dst_ref=rt.at[row], send_sem=row_send.at[t], recv_sem=row_recv.at[row],
                device_id={"lat": (row + t) * ROW + col}, device_id_type=MESH,
            ).start()

    def recurse(v):
        w = jnp.zeros((L, I), f32)
        for j in range(J):
            w = sl[v, j] + sf[v, j] * column(incoming[v], j) + nb[v, j] * w
            wb[v, j] = w * column(scale[v], j)

    recurse(0)
    inside[...] = jnp.zeros_like(inside)
    for r in range(ROWS - 1):

        @pl.when(r < row)
        def _():
            pltpu.make_async_copy(rt.at[r], rt.at[r], row_recv.at[r]).wait()
            inside[...] = rt[r] + gt[r] * inside[...]

    carry = inside[...]
    for c in range(ROW):
        s4[c] = carry
        along_row(s4, r4, c, c, send_sem.at[3], recv_sem.at[3])
        if c + 1 < ROW:
            carry = r3[c] + gb[ROW * row + c] * carry
    recurse(1)
    wait(r4, recv_sem.at[3])
    for v in range(V):
        for h in range(2):
            inflow[v, Q * h : Q * h + Q] = r4[2 * v + h]
    for t in range(1, ROWS):

        @pl.when(row + t < ROWS)
        def _():
            pltpu.make_async_copy(st, st, row_send.at[t]).wait()

    wait(spikes.at[pl.ds(0, LON - 1)], send_sem.at[0])
    wait(ends.at[pl.ds(0, LON - 1)], send_sem.at[1])
    wait(s3.at[pl.ds(0, ROW - 1)], send_sem.at[2])
    wait(s4.at[pl.ds(0, ROW - 1)], send_sem.at[3])


def finish(wb, inflow, extent, mixing, out_hbm, ob, out_sem):
    oflat = ob.reshape(V * 3 * L * 8, I)
    stores = []
    for v in range(V):
        carry = inflow[v]
        for j in range(0, J, 2):
            his, los = [], []
            for jj in (j, j + 1):
                m = wb[v, jj] + column(extent[v], jj) * carry
                hi = m.astype(jnp.bfloat16)
                his.append(hi)
                los.append((m - hi.astype(f32)).astype(jnp.bfloat16))
            hi = jnp.concatenate(his, axis=1)
            lo = jnp.concatenate(los, axis=1)
            y = jnp.dot(mixing[v], jnp.concatenate([hi, lo, hi], axis=0), preferred_element_type=f32)
            for n, jj in enumerate((j, j + 1)):
                oflat[pl.ds((3 * v + jj // 8) * L * 8 + jj % 8, L, stride=8), :] = y[:, I * n : I * n + I]
            if j % 8 == 6:
                n = 3 * v + j // 8
                store = pltpu.make_async_copy(ob.at[n], out_hbm.at[v, :, pl.ds(8 * (j // 8), 8), :], out_sem.at[n])
                store.start()
                stores.append(store)
    for store in stores:
        store.wait()


def shards(increment, eastward_rate, eastward_spike, northward_rate, vertical):
    anywhere = pl.BlockSpec(memory_space=pltpu.HBM)
    vm = pltpu.VMEM
    here = pl.BlockSpec(memory_space=pltpu.VMEM)
    held = [
        pltpu.with_memory_space_constraint(a, pltpu.HBM)
        for a in (increment, eastward_rate.transpose(0, 2, 1), eastward_spike, northward_rate, vertical)
    ]
    parts = pl.pallas_call(
        kernel,
        out_shape=[
            vm((V, J, L, I), f32),
            vm((V, L, I), f32),
            vm((V, L, I), f32),
            vm((V, L, 3 * L), jnp.bfloat16),
        ],
        in_specs=[anywhere] * 5,
        out_specs=[here] * 4,
        scratch_shapes=[
            vm((V * 3, L, 8, I), f32),
            vm((V, J, L), f32),
            vm((J, I), f32),
            vm((V, L, J * LAT), f32),
            vm((V, L, L), f32),
            vm((V, L, I), f32),
            vm((V, L, I), f32),
            vm((7, J, I), f32),
            vm((J, I), f32),
            vm((J, I), f32),
            vm((V, J, L, I), f32),
            vm((V, J, L, I), f32),
            vm((V, J, L, I), f32),
            vm((LAT, Q, I), f32),
            vm((ROWS, Q, I), f32),
            vm((8, L, I), f32),
            vm((8, L, I), f32),
            vm((V, L, I), f32),
            vm((V, L, I), f32),
            vm((V, L, I), f32),
            vm((3, 8, I), f32),
            vm((LON, 1, I), f32),
            vm((3, LON, I), f32),
            vm((LON, 3, 8, I), f32),
            vm((ROW, Q, I), f32),
            vm((ROW, Q, I), f32),
            vm((Q, I), f32),
            vm((ROWS, Q, I), f32),
            vm((Q, I), f32),
            vm((ROW, Q, I), f32),
            vm((ROW, Q, I), f32),
            pltpu.SemaphoreType.DMA((10,)),
            pltpu.SemaphoreType.DMA((4,)),
            pltpu.SemaphoreType.DMA((4,)),
            pltpu.SemaphoreType.DMA((ROWS,)),
            pltpu.SemaphoreType.DMA((ROWS,)),
        ],
        compiler_params=pltpu.CompilerParams(
            collective_id=0, has_side_effects=True, vmem_limit_bytes=48 * 1024 * 1024
        ),
    )(*held)
    return pl.pallas_call(
        finish,
        out_shape=jax.ShapeDtypeStruct((V, L, J, I), f32),
        in_specs=[here] * 4,
        out_specs=anywhere,
        scratch_shapes=[vm((V * 3, L, 8, I), f32), pltpu.SemaphoreType.DMA((6,))],
        compiler_params=pltpu.CompilerParams(vmem_limit_bytes=48 * 1024 * 1024),
    )(*parts)


def solution(mesh):
    return jax.shard_map(
        shards,
        mesh=mesh,
        in_specs=(P(None, None, "lat", "lon"), P(None, None, "lat"), P("lat", "lon"), P(), P()),
        out_specs=P(None, None, "lat", "lon"),
        check_vma=False,
    )
```
